32 devices in a mesh: grp: 2 (over y), frm: 4 (over z), row: 4 (over x, core).
Axes of the slice: x: 2, y: 2, z: 4, core: 2. Of those that a mesh axis runs over, the one named last changes fastest.
Arguments:
- hidden_in: bfloat16 [512, 16, 2240], P('row', ('grp', 'frm')), parts along dimension 1, may hold values from -6 to 6
- norm_gain: float32 [2240], replicated, may hold values from 0.1 to 1.9
- query_key_value_weight: bfloat16 [2240, 3, 2240], P(None, None, 'row'), may hold values from -0.125 to 0.125
- head_gain: float32 [2240], P('row'), may hold values from 0.1 to 1.9
- output_matrix: bfloat16 [2240, 2240], P('row'), may hold values from -0.125 to 0.125
- block_end: int32 [16], P(('grp', 'frm')), parts along dimension 0, may hold values from 0 to 7, as said below
Outputs:
- mixed_out: bfloat16 [512, 16, 2240], P('row', ('grp', 'frm')), parts along dimension 1
The draws below stay inside these ranges and needn't reach their ends.
There are 2 independent parts, one for each index of `grp`. The reference program is written for one: setup_inputs(seed, part) draws one part's arguments, and reference() takes and returns one part's arrays. A program takes and returns all parts, laid end to end along the dimension named above; an argument that names none is the same for every part. Nothing has to cross between parts.
Inputs may be any that keep to these rules, and one draw needn't show every extreme that they name: `block_end`: entries never fall from one frame to the next; each entry is at least its frame's index, and frames with equal entries form a block of consecutive frames; a block never holds frames of two different runs of 2 frames (f // 2 differs), and the last frame of every such run ends a block.
All inputs are finite; a program needn't handle non-finite values.
Results may differ from the reference program's by a relative error of at most 0.015.
Values may be sent and summed in bfloat16 or wider, within the bound.
A program may use at most 64 MiB of HBM per device.

```python
import jax
import jax.numpy as jnp
from jax import lax

D = 2240
HEADS = 20
HD = 112
FH = 16
FW = 32
FR_DEV = 2
FRAMES = 8
N_ROW = 4


def draw_block_end(key, part):
    frame_index = jnp.arange(FRAMES, dtype=jnp.int32)
    coins = jax.random.randint(jax.random.fold_in(key, 7), (FRAMES,), 0, 2, dtype=jnp.int32)
    starts = jnp.where(frame_index % FR_DEV == 0, 1, coins)
    block_ident = jnp.cumsum(starts) - 1
    same_block = block_ident[None, :] == block_ident[:, None]
    return jnp.max(jnp.where(same_block, frame_index[None, :], -1), axis=1).astype(jnp.int32)


def level_of(key, dims, split, smallest, high):
    factor_of = 1.0
    for dim, blocks in split:
        heights = jax.random.uniform(jax.random.fold_in(jax.random.fold_in(key, 6), dim), (blocks,), jnp.float32, smallest / len(split), high / len(split))
        factor_of = factor_of * jnp.repeat(jnp.exp(heights), dims[dim] // blocks).reshape((-1,) + (1,) * (len(dims) - 1 - dim))
    return factor_of


def noise(stream_key, extent, width, most, split=(), kind=jnp.bfloat16):
    drawn = jax.random.normal(stream_key, extent, jnp.float32) * width
    if len(split) > 0:
        drawn = level_of(stream_key, extent, split, -0.22, 0.18) * drawn
    return jnp.clip(drawn, min=-most, max=most).astype(kind)


def setup_inputs(seed: int = 0, part: int = 0) -> dict:
    seeds = jax.random.split(jax.random.key(seed), 7)
    own_keys = jax.random.split(jax.random.fold_in(seeds[6], part), 7)
    return {
        "hidden_in": noise(own_keys[0], (FH * FW, FRAMES, D), 1.0, 6.0, ((0, 4), (1, 4))),
        "norm_gain": jnp.clip(1.0 + 0.18 * jax.random.normal(seeds[1], (D,), jnp.float32), 0.1, 1.9),
        "query_key_value_weight": noise(seeds[2], (D, 3, HEADS * HD), D ** -0.5, 0.125, ((2, 4),)),
        "head_gain": jnp.clip(1.0 + 0.18 * jax.random.normal(seeds[3], (HEADS * HD,), jnp.float32), 0.1, 1.9),
        "output_matrix": noise(seeds[4], (HEADS * HD, D), (HEADS * HD) ** -0.5, 0.125, ((0, 4),)),
        "block_end": draw_block_end(jax.random.fold_in(jax.random.fold_in(seeds[6], part), 71), part),
    }


epsilon = 1e-06

def reference(hidden_in, norm_gain, query_key_value_weight, head_gain, output_matrix, block_end):
    positions = FH * FW
    as_float = hidden_in.astype(jnp.float32)
    mean_square = lax.optimization_barrier(jnp.mean(as_float * as_float, axis=-1, keepdims=True))
    normed = (as_float * lax.rsqrt(mean_square + epsilon) * norm_gain).astype(jnp.bfloat16)
    weights = query_key_value_weight.reshape(D, 3 * HEADS * HD)
    projected = jnp.dot(normed.reshape(positions * FRAMES, D), weights, preferred_element_type=jnp.float32).astype(jnp.bfloat16)
    projected = projected.reshape(positions, FRAMES, 3, HEADS, HD)
    queries = jax.nn.relu(projected[:, :, 0]).astype(jnp.float32)
    key_relu = jax.nn.relu(projected[:, :, 1]).astype(jnp.float32)
    values = projected[:, :, 2].astype(jnp.float32)
    per_frame_state = jnp.einsum('pfhi,pfhj->fhij', key_relu, values, precision=lax.Precision.HIGHEST)
    earlier_mask = (block_end[None, :] <= block_end[:, None]).astype(jnp.float32)
    block_state = jnp.einsum('fg,ghij->fhij', earlier_mask, per_frame_state, precision=lax.Precision.HIGHEST).astype(jnp.bfloat16)
    attended = jnp.einsum('pfhi,fhij->pfhj', queries, block_state.astype(jnp.float32), precision=lax.Precision.HIGHEST)
    head_square = lax.optimization_barrier(jnp.mean(attended * attended, axis=-1, keepdims=True))
    head_out = (attended * lax.rsqrt(head_square + epsilon) * head_gain.reshape(HEADS, HD)).astype(jnp.bfloat16)
    merged_heads = head_out.reshape(positions * FRAMES, HEADS * HD)
    group_width = HEADS * HD // N_ROW
    summed = jnp.zeros((positions * FRAMES, D), jnp.float32)
    for group in range(N_ROW):
        head_cols = merged_heads[:, group * group_width:(group + 1) * group_width]
        weight_part = output_matrix[group * group_width:(group + 1) * group_width]
        partial_term = jnp.dot(head_cols, weight_part, preferred_element_type=jnp.float32)
        rounded = lax.optimization_barrier(partial_term.astype(jnp.bfloat16)).astype(jnp.float32)
        summed = summed + rounded
    return summed.astype(jnp.bfloat16).reshape(positions, FRAMES, D)
```

```python
import functools

import jax
import jax.numpy as jnp
from jax import lax
from jax.experimental import pallas as pl
from jax.experimental.pallas import tpu as pltpu
from jax.sharding import PartitionSpec as P

HD = 112
LANES = 128
PARTS = 3
QUERY, KEY, VALUE = 0, 1, 2

epsilon = 1e-06


def slices_of(rows, wanted):
    count = wanted
    while rows % count or (rows // count) % 16:
        count -= 1
    return count, rows // count


def kernel(
    n_row, n_frm,
    hid, ng, w_hbm, hg, wo_hbm, block_end,
    out,
    xg, w, wo, wot, proj, st, chain_s, prior, ho_c, ho_o, hs_c, hs_o, red_s, red_r,
    w_sem, wo_sem, wx_s, wx_r, gp_s, gp_r, gx_s, gx_r, gf_s, gf_r, ch_s, ch_r, he_s, he_r, rd_s, rd_r,
):
    frames, width, slab = hid.shape
    group_width = w.shape[1]
    heads = group_width // HD
    me = lax.axis_index("row")
    fi = lax.axis_index("frm")
    mate = me + 1 - 2 * lax.rem(me, 2)
    cross = lax.rem(me + 2, n_row)

    def remote(src, dst, s, r, **where):
        return pltpu.make_async_remote_copy(
            src_ref=src, dst_ref=dst, send_sem=s, recv_sem=r,
            device_id=where, device_id_type=pl.DeviceIdType.MESH,
        )

    barrier = pltpu.get_barrier_semaphore()
    for where in (
        {"row": mate}, {"row": cross},
        {"frm": lax.rem(fi + 1, n_frm)}, {"frm": lax.rem(fi + n_frm - 1, n_frm)},
    ):
        pl.semaphore_signal(barrier, inc=1, device_id=where, device_id_type=pl.DeviceIdType.MESH)

    w_copies = {}
    for part in (KEY, VALUE, QUERY):
        w_copies[part] = pltpu.make_async_copy(w_hbm.at[part], w.at[part], w_sem.at[part])
        w_copies[part].start()
    wo_copy = pltpu.make_async_copy(wo_hbm, wo.at[pl.ds(0, group_width)], wo_sem.at[0])
    wo_copy.start()

    norm_steps, norm_rows = slices_of(width, 14)

    def norm(f):
        def squares(i, acc):
            rows = pl.ds(pl.multiple_of(i * norm_rows, 16), norm_rows)
            v = hid[f, rows, :].astype(jnp.float32)
            return acc + jnp.sum((v * v).reshape(norm_rows // 8, 8, slab), axis=0)

        acc = lax.fori_loop(0, norm_steps, squares, jnp.zeros((8, slab), jnp.float32))
        scale = lax.rsqrt(jnp.sum(acc, axis=0, keepdims=True) / width + epsilon)

        def write(i, carry):
            rows = pl.ds(pl.multiple_of(i * norm_rows, 16), norm_rows)
            v = hid[f, rows, :].astype(jnp.float32)
            xg[0, f, rows, :] = (v * scale * ng[rows, :]).astype(jnp.bfloat16)
            return carry

        lax.fori_loop(0, norm_steps, write, 0)

    to_mate, to_cross, forward = [], [], []
    for f in range(frames):
        to_mate.append(remote(xg.at[0, f], xg.at[1, f], gp_s.at[f], gp_r.at[f], row=mate))
        to_cross.append(remote(xg.at[0, f], xg.at[2, f], gx_s.at[f], gx_r.at[f], row=cross))
        forward.append(remote(xg.at[2, f], xg.at[3, f], gf_s.at[f], gf_r.at[f], row=mate))
    wo_exchange = remote(
        wo_hbm, wo.at[pl.ds(group_width, group_width)], wx_s.at[0], wx_r.at[0], row=mate
    )

    for f in range(frames):
        norm(f)
        if f == 0:
            pl.semaphore_wait(barrier, 4)
        to_cross[f].start()
        to_mate[f].start()
    wo_exchange.start()

    def project(f, first, part):
        tokens = jnp.concatenate([xg[first, f], xg[first + 1, f]], axis=1)
        r = jnp.dot(w[part], tokens, preferred_element_type=jnp.float32)
        if part != VALUE:
            r = jnp.maximum(r, 0.0)
        proj[f, part, :, pl.ds(first * slab, 2 * slab)] = r.astype(jnp.bfloat16)

    def add_state(f, first):
        for h in range(heads):
            rows, cols = pl.ds(h * HD, HD), pl.ds(first * slab, 2 * slab)
            s = lax.dot_general(
                proj[f, VALUE, rows, cols], proj[f, KEY, rows, cols],
                (((1,), (1,)), ((), ())), preferred_element_type=jnp.float32,
            )
            if first == 0:
                st[f, h] = s
            else:
                st[f, h] += s

    for f in range(frames):
        to_mate[f].wait_recv()
        for part in (KEY, VALUE, QUERY):
            if f == 0:
                w_copies[part].wait()
            project(f, 0, part)
        add_state(f, 0)

    def transpose_rows(start, count):
        wot[:, pl.ds(start, count)] = wo[pl.ds(start, count), :].T

    wo_copy.wait()
    wo_exchange.wait_recv()

    def flip(i, carry):
        rows = pl.ds(pl.multiple_of(i * LANES, LANES), LANES)
        wot[:, rows] = wo[rows, :].T
        return carry

    whole = 2 * group_width // LANES
    lax.fori_loop(0, whole, flip, 0)
    if 2 * group_width % LANES:
        transpose_rows(whole * LANES, 2 * group_width % LANES)

    for f in range(frames):
        to_cross[f].wait_recv()
        forward[f].start()
        forward[f].wait_recv()
        project(f, 2, KEY)
        project(f, 2, VALUE)
        if f < frames - 1:
            project(f, 2, QUERY)
        add_state(f, 2)

    chain = [
        remote(chain_s.at[h], prior.at[h], ch_s.at[h], ch_r.at[h], frm=lax.rem(fi + 1, n_frm))
        for h in range(heads)
    ]

    def own_sum(h):
        total = st[0, h]
        for f in range(1, frames):
            total = total + st[f, h]
        return total

    @pl.when(fi == 0)
    def _():
        for h in range(heads):
            chain_s[h] = own_sum(h).astype(jnp.bfloat16)
            chain[h].start()
        prior[...] = jnp.zeros_like(prior)

    project(frames - 1, 2, QUERY)

    @pl.when(fi > 0)
    def _():
        for h in range(heads):
            chain[h].wait_recv()

            @pl.when(fi < n_frm - 1)
            def _():
                chain_s[h] = (prior[h].astype(jnp.float32) + own_sum(h)).astype(jnp.bfloat16)
                chain[h].start()

    def attend(first, keep, give):
        cols = pl.ds(first * slab, 2 * slab)
        for f in range(frames):
            for h in range(heads):
                rows = pl.ds(h * HD, HD)
                total = prior[h].astype(jnp.float32)
                for g in range(frames):
                    use = jnp.where(block_end[g] <= block_end[f], 1.0, 0.0)
                    total = total + use * st[g, h]
                a = jnp.dot(
                    total.astype(jnp.bfloat16), proj[f, QUERY, rows, cols],
                    preferred_element_type=jnp.float32,
                )
                scale = lax.rsqrt(jnp.mean(a * a, axis=0, keepdims=True) + epsilon)
                a = a * scale
                gain = hg[rows, :]
                keep[rows, pl.ds(f * slab, slab)] = (a[:, :slab] * gain).astype(jnp.bfloat16)
                give[rows, pl.ds(f * slab, slab)] = (a[:, slab:] * gain).astype(jnp.bfloat16)

    swap_c = remote(hs_c, ho_c.at[pl.ds(group_width, group_width)], he_s.at[0], he_r.at[0], row=mate)
    swap_o = remote(hs_o, ho_o.at[pl.ds(group_width, group_width)], he_s.at[1], he_r.at[1], row=mate)
    attend(2, ho_c, hs_c)
    swap_c.start()
    attend(0, ho_o, hs_o)
    swap_o.start()
    swap_c.wait_recv()

    n_red = rd_s.shape[0]
    red_rows = width // n_red
    reduce = []
    for i in range(n_red):
        rows = pl.ds(i * red_rows, red_rows)
        r = jnp.dot(wot[rows, :], ho_c[...], preferred_element_type=jnp.float32)
        for f in range(frames):
            red_s[f, rows, :] = r[:, f * slab:(f + 1) * slab].astype(jnp.bfloat16)
        reduce.append(remote(
            red_s.at[:, rows, :], red_r.at[:, rows, :], rd_s.at[i], rd_r.at[i], row=cross
        ))
        reduce[i].start()

    swap_o.wait_recv()
    for i in range(n_red):
        rows = pl.ds(i * red_rows, red_rows)
        r = jnp.dot(wot[rows, :], ho_o[...], preferred_element_type=jnp.float32)
        reduce[i].wait_recv()
        for f in range(frames):
            other = red_r[f, rows, :].astype(jnp.float32)
            out[f, rows, :] = (r[:, f * slab:(f + 1) * slab] + other).astype(jnp.bfloat16)

    for copy in to_mate + to_cross + forward + [wo_exchange, swap_c, swap_o] + reduce:
        copy.wait_send()

    @pl.when(fi < n_frm - 1)
    def _():
        for h in range(heads):
            chain[h].wait_send()


def per_device(n_row, n_frm, hidden_in, norm_gain, query_key_value_weight, head_gain, output_matrix, block_end):
    slab, frames, width = hidden_in.shape
    group_width = head_gain.shape[0]
    heads = group_width // HD
    bf16, f32 = jnp.bfloat16, jnp.float32
    n_red, _ = slices_of(width, 5)
    vmem = pl.BlockSpec(memory_space=pltpu.VMEM)
    hbm = pl.BlockSpec(memory_space=pl.ANY)
    smem = pl.BlockSpec(memory_space=pltpu.SMEM)
    dma = pltpu.SemaphoreType.DMA
    result = pl.pallas_call(
        functools.partial(kernel, n_row, n_frm),
        out_shape=jax.ShapeDtypeStruct((frames, width, slab), bf16),
        in_specs=[vmem, vmem, hbm, vmem, hbm, smem],
        out_specs=vmem,
        scratch_shapes=[
            pltpu.VMEM((n_row, frames, width, slab), bf16),
            pltpu.VMEM((PARTS, group_width, width), bf16),
            pltpu.VMEM((2 * group_width, width), bf16),
            pltpu.VMEM((width, 2 * group_width), bf16),
            pltpu.VMEM((frames, PARTS, group_width, n_row * slab), bf16),
            pltpu.VMEM((frames, heads, HD, HD), f32),
            pltpu.VMEM((heads, HD, HD), bf16),
            pltpu.VMEM((heads, HD, HD), bf16),
            pltpu.VMEM((2 * group_width, frames * slab), bf16),
            pltpu.VMEM((2 * group_width, frames * slab), bf16),
            pltpu.VMEM((group_width, frames * slab), bf16),
            pltpu.VMEM((group_width, frames * slab), bf16),
            pltpu.VMEM((frames, width, slab), bf16),
            pltpu.VMEM((frames, width, slab), bf16),
            dma((PARTS,)), dma((1,)), dma((1,)), dma((1,)),
            dma((frames,)), dma((frames,)), dma((frames,)), dma((frames,)),
            dma((frames,)), dma((frames,)),
            dma((heads,)), dma((heads,)), dma((2,)), dma((2,)),
            dma((n_red,)), dma((n_red,)),
        ],
        compiler_params=pltpu.CompilerParams(
            collective_id=0, has_side_effects=True, vmem_limit_bytes=60 * 1024 * 1024
        ),
        name="layer",
    )(
        hidden_in.transpose(1, 2, 0),
        jnp.broadcast_to(norm_gain[:, None], (width, slab)),
        query_key_value_weight.transpose(1, 2, 0),
        jnp.broadcast_to(head_gain[:, None], (group_width, slab)),
        output_matrix,
        block_end,
    )
    return result.transpose(2, 0, 1)


def solution(mesh):
    placed = (
        P("row", ("grp", "frm"), None),
        P(),
        P(None, None, "row"),
        P("row"),
        P("row", None),
        P(("grp", "frm")),
    )
    return jax.shard_map(
        functools.partial(per_device, mesh.shape["row"], mesh.shape["frm"]),
        mesh=mesh,
        in_specs=placed,
        out_specs=P("row", ("grp", "frm"), None),
        check_vma=False,
    )
```

```python
import functools

import jax
import jax.numpy as jnp
from jax import lax
from jax.experimental import pallas as pl
from jax.experimental.pallas import tpu as pltpu
from jax.sharding import PartitionSpec as P

HD = 112
LANES = 128
PARTS = 3
QUERY, KEY, VALUE = 0, 1, 2

epsilon = 1e-06


def slices_of(rows, wanted):
    count = wanted
    while rows % count or (rows // count) % 16:
        count -= 1
    return count, rows // count


def kernel(
    n_row, n_frm,
    hid, ng, w_hbm, hg, wo_hbm, block_end,
    out,
    ng_c, hg_c, xg, w, wo, wot, proj, st, chain_s, prior, ho_c, ho_o, hs_c, hs_o, red_s, red_r,
    w_sem, wo_sem, wx_s, wx_r, gp_s, gp_r, gx_s, gx_r, gf_s, gf_r, ch_s, ch_r, he_s, he_r, rd_s, rd_r,
):
    frames, width, slab = hid.shape
    group_width = w.shape[1]
    heads = group_width // HD
    me = lax.axis_index("row")
    fi = lax.axis_index("frm")
    mate = me + 1 - 2 * lax.rem(me, 2)
    cross = lax.rem(me + 2, n_row)

    def remote(src, dst, s, r, **where):
        return pltpu.make_async_remote_copy(
            src_ref=src, dst_ref=dst, send_sem=s, recv_sem=r,
            device_id=where, device_id_type=pl.DeviceIdType.MESH,
        )

    barrier = pltpu.get_barrier_semaphore()
    for where in (
        {"row": mate}, {"row": cross},
        {"frm": lax.rem(fi + 1, n_frm)}, {"frm": lax.rem(fi + n_frm - 1, n_frm)},
    ):
        pl.semaphore_signal(barrier, inc=1, device_id=where, device_id_type=pl.DeviceIdType.MESH)

    w_copies = {}
    for part in (KEY, VALUE, QUERY):
        w_copies[part] = pltpu.make_async_copy(w_hbm.at[part], w.at[part], w_sem.at[part])
        w_copies[part].start()
    wo_copy = pltpu.make_async_copy(wo_hbm, wo.at[pl.ds(0, group_width)], wo_sem.at[0])
    wo_copy.start()

    def as_column(row, column):
        for start in range(0, column.shape[0], LANES):
            count = min(LANES, column.shape[0] - start)
            spread = jnp.broadcast_to(row[:, pl.ds(start, count)], (LANES, count))
            column[pl.ds(start, count), :] = spread.T

    as_column(ng, ng_c)
    norm_steps, norm_rows = slices_of(width, 14)

    def norm(f):
        def squares(i, acc):
            rows = pl.ds(pl.multiple_of(i * norm_rows, 16), norm_rows)
            v = hid[f, rows, :].astype(jnp.float32)
            return acc + jnp.sum((v * v).reshape(norm_rows // 8, 8, slab), axis=0)

        acc = lax.fori_loop(0, norm_steps, squares, jnp.zeros((8, slab), jnp.float32))
        scale = lax.rsqrt(jnp.sum(acc, axis=0, keepdims=True) / width + epsilon)

        def write(i, carry):
            rows = pl.ds(pl.multiple_of(i * norm_rows, 16), norm_rows)
            v = hid[f, rows, :].astype(jnp.float32)
            xg[0, f, rows, :] = (v * scale * ng_c[rows, :]).astype(jnp.bfloat16)
            return carry

        lax.fori_loop(0, norm_steps, write, 0)

    to_mate, to_cross, forward = [], [], []
    n_cut, cut_rows = slices_of(width, 4)
    for f in range(frames):
        to_mate.append(remote(xg.at[0, f], xg.at[1, f], gp_s.at[f], gp_r.at[f], row=mate))
        for k in range(n_cut):
            rows, i = pl.ds(k * cut_rows, cut_rows), f * n_cut + k
            to_cross.append(remote(
                xg.at[0, f, rows], xg.at[2, f, rows], gx_s.at[i], gx_r.at[i], row=cross
            ))
            forward.append(remote(
                xg.at[2, f, rows], xg.at[3, f, rows], gf_s.at[i], gf_r.at[i], row=mate
            ))
    wo_exchange = remote(
        wo_hbm, wo.at[pl.ds(group_width, group_width)], wx_s.at[0], wx_r.at[0], row=mate
    )

    for f in range(frames):
        norm(f)
        if f == 0:
            pl.semaphore_wait(barrier, 4)
        for k in range(n_cut):
            to_cross[f * n_cut + k].start()
        to_mate[f].start()
    wo_exchange.start()

    def project(f, first, part):
        tokens = jnp.concatenate([xg[first, f], xg[first + 1, f]], axis=1)
        r = jnp.dot(w[part], tokens, preferred_element_type=jnp.float32)
        if part != VALUE:
            r = jnp.maximum(r, 0.0)
        proj[f, part, :, pl.ds(first * slab, 2 * slab)] = r.astype(jnp.bfloat16)

    def add_state(f, first):
        for h in range(heads):
            rows, cols = pl.ds(h * HD, HD), pl.ds(first * slab, 2 * slab)
            s = lax.dot_general(
                proj[f, VALUE, rows, cols], proj[f, KEY, rows, cols],
                (((1,), (1,)), ((), ())), preferred_element_type=jnp.float32,
            )
            if first == 0:
                st[f, h] = s
            else:
                st[f, h] += s

    for f in range(frames):
        to_mate[f].wait_recv()
        for part in (KEY, VALUE, QUERY):
            if f == 0:
                w_copies[part].wait()
            project(f, 0, part)
        add_state(f, 0)

    def transpose_rows(start, count):
        wot[:, pl.ds(start, count)] = wo[pl.ds(start, count), :].T

    as_column(hg, hg_c)
    wo_copy.wait()
    wo_exchange.wait_recv()

    def flip(i, carry):
        rows = pl.ds(pl.multiple_of(i * LANES, LANES), LANES)
        wot[:, rows] = wo[rows, :].T
        return carry

    whole = 2 * group_width // LANES
    lax.fori_loop(0, whole, flip, 0)
    if 2 * group_width % LANES:
        transpose_rows(whole * LANES, 2 * group_width % LANES)

    for f in range(frames):
        for k in range(f * n_cut, (f + 1) * n_cut):
            to_cross[k].wait_recv()
            forward[k].start()
        for k in range(f * n_cut, (f + 1) * n_cut):
            forward[k].wait_recv()
        project(f, 2, KEY)
        project(f, 2, VALUE)
        if f < frames - 1:
            project(f, 2, QUERY)
        add_state(f, 2)

    chain = [
        remote(chain_s.at[h], prior.at[h], ch_s.at[h], ch_r.at[h], frm=lax.rem(fi + 1, n_frm))
        for h in range(heads)
    ]

    def own_sum(h):
        total = st[0, h]
        for f in range(1, frames):
            total = total + st[f, h]
        return total

    @pl.when(fi == 0)
    def _():
        for h in range(heads):
            chain_s[h] = own_sum(h).astype(jnp.bfloat16)
            chain[h].start()
        prior[...] = jnp.zeros_like(prior)

    project(frames - 1, 2, QUERY)

    @pl.when(fi > 0)
    def _():
        for h in range(heads):
            chain[h].wait_recv()

            @pl.when(fi < n_frm - 1)
            def _():
                chain_s[h] = (prior[h].astype(jnp.float32) + own_sum(h)).astype(jnp.bfloat16)
                chain[h].start()

    def attend(first, keep, give):
        cols = pl.ds(first * slab, 2 * slab)
        for f in range(frames):
            for h in range(heads):
                rows = pl.ds(h * HD, HD)
                total = prior[h].astype(jnp.float32)
                for g in range(frames):
                    use = jnp.where(block_end[g] <= block_end[f], 1.0, 0.0)
                    total = total + use * st[g, h]
                a = jnp.dot(
                    total.astype(jnp.bfloat16), proj[f, QUERY, rows, cols],
                    preferred_element_type=jnp.float32,
                )
                scale = lax.rsqrt(jnp.mean(a * a, axis=0, keepdims=True) + epsilon)
                a = a * scale
                gain = hg_c[rows, :]
                keep[rows, pl.ds(f * slab, slab)] = (a[:, :slab] * gain).astype(jnp.bfloat16)
                give[rows, pl.ds(f * slab, slab)] = (a[:, slab:] * gain).astype(jnp.bfloat16)

    swap_c = remote(hs_c, ho_c.at[pl.ds(group_width, group_width)], he_s.at[0], he_r.at[0], row=mate)
    swap_o = remote(hs_o, ho_o.at[pl.ds(group_width, group_width)], he_s.at[1], he_r.at[1], row=mate)
    attend(2, ho_c, hs_c)
    swap_c.start()
    attend(0, ho_o, hs_o)
    swap_o.start()
    swap_c.wait_recv()

    n_red = rd_s.shape[0]
    red_rows = width // n_red
    reduce = []
    for i in range(n_red):
        rows = pl.ds(i * red_rows, red_rows)
        r = jnp.dot(wot[rows, :], ho_c[...], preferred_element_type=jnp.float32)
        for f in range(frames):
            red_s[f, rows, :] = r[:, f * slab:(f + 1) * slab].astype(jnp.bfloat16)
        reduce.append(remote(
            red_s.at[:, rows, :], red_r.at[:, rows, :], rd_s.at[i], rd_r.at[i], row=cross
        ))
        reduce[i].start()

    swap_o.wait_recv()
    for i in range(n_red):
        rows = pl.ds(i * red_rows, red_rows)
        r = jnp.dot(wot[rows, :], ho_o[...], preferred_element_type=jnp.float32)
        reduce[i].wait_recv()
        for f in range(frames):
            other = red_r[f, rows, :].astype(jnp.float32)
            out[f, rows, :] = (r[:, f * slab:(f + 1) * slab] + other).astype(jnp.bfloat16)

    for copy in to_mate + to_cross + forward + [wo_exchange, swap_c, swap_o] + reduce:
        copy.wait_send()

    @pl.when(fi < n_frm - 1)
    def _():
        for h in range(heads):
            chain[h].wait_send()


def per_device(n_row, n_frm, hidden_in, norm_gain, query_key_value_weight, head_gain, output_matrix, block_end):
    slab, frames, width = hidden_in.shape
    group_width = head_gain.shape[0]
    heads = group_width // HD
    bf16, f32 = jnp.bfloat16, jnp.float32
    n_red, _ = slices_of(width, 7)
    n_cut, _ = slices_of(width, 4)
    vmem = pl.BlockSpec(memory_space=pltpu.VMEM)
    hbm = pl.BlockSpec(memory_space=pl.ANY)
    smem = pl.BlockSpec(memory_space=pltpu.SMEM)
    dma = pltpu.SemaphoreType.DMA
    result = pl.pallas_call(
        functools.partial(kernel, n_row, n_frm),
        out_shape=jax.ShapeDtypeStruct((frames, width, slab), bf16),
        in_specs=[vmem, vmem, hbm, vmem, hbm, smem],
        out_specs=vmem,
        scratch_shapes=[
            pltpu.VMEM((width, slab), f32),
            pltpu.VMEM((group_width, slab), f32),
            pltpu.VMEM((n_row, frames, width, slab), bf16),
            pltpu.VMEM((PARTS, group_width, width), bf16),
            pltpu.VMEM((2 * group_width, width), bf16),
            pltpu.VMEM((width, 2 * group_width), bf16),
            pltpu.VMEM((frames, PARTS, group_width, n_row * slab), bf16),
            pltpu.VMEM((frames, heads, HD, HD), f32),
            pltpu.VMEM((heads, HD, HD), bf16),
            pltpu.VMEM((heads, HD, HD), bf16),
            pltpu.VMEM((2 * group_width, frames * slab), bf16),
            pltpu.VMEM((2 * group_width, frames * slab), bf16),
            pltpu.VMEM((group_width, frames * slab), bf16),
            pltpu.VMEM((group_width, frames * slab), bf16),
            pltpu.VMEM((frames, width, slab), bf16),
            pltpu.VMEM((frames, width, slab), bf16),
            dma((PARTS,)), dma((1,)), dma((1,)), dma((1,)),
            dma((frames,)), dma((frames,)),
            *[dma((frames * n_cut,)) for _ in range(4)],
            dma((heads,)), dma((heads,)), dma((2,)), dma((2,)),
            dma((n_red,)), dma((n_red,)),
        ],
        compiler_params=pltpu.CompilerParams(
            collective_id=0, has_side_effects=True, vmem_limit_bytes=60 * 1024 * 1024
        ),
        name="layer",
    )(
        hidden_in.transpose(1, 2, 0),
        norm_gain[None, :],
        query_key_value_weight.transpose(1, 2, 0),
        head_gain[None, :],
        output_matrix,
        block_end,
    )
    return result.transpose(2, 0, 1)


def solution(mesh):
    placed = (
        P("row", ("grp", "frm"), None),
        P(),
        P(None, None, "row"),
        P("row"),
        P("row", None),
        P(("grp", "frm")),
    )
    return jax.shard_map(
        functools.partial(per_device, mesh.shape["row"], mesh.shape["frm"]),
        mesh=mesh,
        in_specs=placed,
        out_specs=P("row", ("grp", "frm"), None),
        check_vma=False,
    )
```
